32 devices in a mesh: fsdp: 8 (over z, y), fac: 4 (over x, core).
Axes of the slice: x: 2, y: 2, z: 4, core: 2. Of those that a mesh axis runs over, the one named last changes fastest.
Arguments:
- activations: bfloat16 [8192, 3072], P('fsdp'), may hold values from -6 to 6
- out_grads: bfloat16 [8192, 3072], P('fsdp', 'fac'), may hold values from -12 to 12
- token_ids: int32 [8192], P('fsdp'), may hold values from 0 to 32767
- forget_mask: int32 [8192], P('fsdp'), may hold values 0 or 1
- importance: float32 [32768], replicated, may hold values from 0.3 to 3
- in_inverse: bfloat16 [3072, 3072], P('fsdp'), may hold values from -1 to 3, as said below
- out_inverse: bfloat16 [3072, 3072], P(None, 'fac'), may hold values from -1 to 3, as said below
Outputs:
- newton_step: float32 [3072, 3072], P('fsdp', 'fac')
- residual: float32 [3072, 3072], P('fsdp', 'fac')
The draws below stay inside these ranges and needn't reach their ends.
Inputs may be any that keep to these rules, and one draw needn't show every extreme that they name: `in_inverse`: symmetric and positive definite. `out_inverse`: symmetric and positive definite.
All inputs are finite; a program needn't handle non-finite values. No bound on the sum of `forget_mask` on one device may be relied on, other than what follows from the above.
Results may differ from the reference program's by a relative error of at most 0.03.
Values may be sent and summed in bfloat16 or wider, within the bound.
A program may use at most 64 MiB of HBM per device.

```python
import math
import jax
import jax.numpy as jnp
import numpy as np
from jax import lax

D_IN = 3072
D_OUT = 3072
VOCAB = 32768
TOK_DEV = 1024
ITERS = 2
TOKENS = 8192
N_FSDP = 8


def symmetric_inverse(key, matrix_order):
    key_noise, key_diag = jax.random.split(key)
    noise_part = jax.random.normal(key_noise, (matrix_order, matrix_order), jnp.float32)
    diag_part = jnp.exp(jax.random.uniform(key_diag, (matrix_order,), jnp.float32, math.log(0.8), math.log(2.0)))
    spread_scale = 0.22 / math.sqrt(matrix_order)
    return jnp.diag(diag_part) + spread_scale * (noise_part + noise_part.T)


def draw_in_inverse(key, part):
    return symmetric_inverse(jax.random.fold_in(key, 11), D_IN).astype(jnp.bfloat16)


def draw_out_inverse(key, part):
    return symmetric_inverse(jax.random.fold_in(key, 23), D_OUT).astype(jnp.bfloat16)


def touch_ends(entries, key, least, largest):
    extent = entries.shape
    place = [jax.random.randint(jax.random.fold_in(key, axis), (), 0, extent[axis]) for axis in range(len(extent))]
    entries = entries.at[tuple(place)].set(least)
    longest = extent.index(max(extent))
    place[longest] = (place[longest] + 1) % extent[longest]
    return entries.at[tuple(place)].set(largest)


def block_levels(key, extent, cuts, least, high):
    def one(position, blocks):
        heights = jax.random.uniform(jax.random.fold_in(jax.random.fold_in(key, 6), position), (blocks,), jnp.float32, least / len(cuts), high / len(cuts))
        return jnp.repeat(jnp.exp(heights), extent[position] // blocks).reshape((-1,) + (1,) * (len(extent) - position - 1))

    loudness = one(*cuts[0])
    for cut in cuts[1:]:
        loudness = loudness * one(*cut)
    return loudness


def cumulative_ranks(number_of, lean):
    portions = [(1 << 20) // math.isqrt(rank ** lean) + 1 for rank in range(1, number_of + 1)]
    width = 1 + sum(portions) // (1 << 30)
    return np.cumsum(np.array([max(1, weight // width) for weight in portions]))


def ranked_ids(own_key, dims, amount, slope):
    listing = cumulative_ranks(amount, slope)
    ticket = jax.random.randint(jax.random.fold_in(own_key, 1), dims, 0, int(listing[amount - 1]))
    rank = jnp.searchsorted(jnp.asarray(listing, jnp.int32), ticket, side="right")
    return jax.random.permutation(jax.random.fold_in(own_key, 2), amount)[rank].astype(jnp.int32)


def gaussian(stream_key, extent, spread, bound, cuts=(), kind=jnp.bfloat16):
    values = jax.random.normal(stream_key, extent, jnp.float32) * spread
    if len(cuts) > 0:
        values = block_levels(stream_key, extent, cuts, -0.22, 0.18) * values
    return jnp.clip(values, min=-bound, max=bound).astype(kind)


def setup_inputs(seed: int = 0) -> dict:
    splits = jax.random.split(jax.random.key(seed), 8)
    return {
        "activations": gaussian(splits[0], (TOKENS, D_IN), 1.0, 6.0, ((0, 8),)),
        "out_grads": gaussian(splits[1], (TOKENS, D_OUT), 2.0, 12.0, ((0, 8), (1, 4))),
        "token_ids": touch_ends(ranked_ids(splits[2], (TOKENS,), VOCAB, 2), jax.random.fold_in(splits[2], 3), 0, VOCAB - 1).astype(jnp.int32),
        "forget_mask": touch_ends((jax.random.randint(splits[3], (TOKENS,), 0, 8) < 1).astype(jnp.int32), jax.random.fold_in(splits[3], 1), 0, 1),
        "importance": jnp.clip(jnp.exp(jax.random.uniform(splits[4], (VOCAB,), jnp.float32, math.log(0.3), math.log(3.0))), 0.3, 3.0),
        "in_inverse": draw_in_inverse(jax.random.fold_in(splits[7], 71), 0),
        "out_inverse": draw_out_inverse(jax.random.fold_in(splits[7], 71), 0),
    }


damping = 0.3

def group_sum(left_groups, right_groups, factor):

    def add_group(carry, pair):
        term = lax.dot_general(pair[0], pair[1], (((0,), (0,)), ((), ())), preferred_element_type=jnp.float32) * factor
        rounded = lax.optimization_barrier(term.astype(jnp.bfloat16))
        return (carry + rounded.astype(jnp.float32), None)
    start_sum = jnp.zeros((left_groups.shape[2], right_groups.shape[2]), jnp.float32)
    summed, unused = lax.scan(add_group, start_sum, (left_groups, right_groups))
    return summed

def reference(activations, out_grads, token_ids, forget_mask, importance, in_inverse, out_inverse):
    keep = 1.0 - forget_mask.astype(jnp.float32)
    weights = importance[token_ids] * keep / TOKENS
    forget_grads = out_grads * forget_mask.astype(jnp.bfloat16)[:, None]
    grouped_acts = activations.reshape(N_FSDP, TOK_DEV, D_IN)
    gradient = group_sum(grouped_acts, forget_grads.reshape(N_FSDP, TOK_DEV, D_OUT), 1.0 / math.sqrt(TOKENS))

    def precondition(matrix):
        mixed = jnp.dot(in_inverse, matrix.astype(jnp.bfloat16), preferred_element_type=jnp.float32)
        return jnp.dot(mixed.astype(jnp.bfloat16), out_inverse, preferred_element_type=jnp.float32)

    def curvature(matrix):
        tok_out = jnp.dot(activations, matrix.astype(jnp.bfloat16), preferred_element_type=jnp.float32)
        scaled = (tok_out * weights[:, None]).astype(jnp.bfloat16)
        return group_sum(grouped_acts, scaled.reshape(N_FSDP, TOK_DEV, D_OUT), 1.0) + damping * matrix
    newton_step = jnp.zeros((D_IN, D_OUT), jnp.float32)
    residual = -gradient
    precond = precondition(residual)
    direction = precond
    inner_now = jnp.sum(residual * precond)
    for iteration in range(ITERS):
        image = curvature(direction)
        alpha = inner_now / jnp.sum(direction * image)
        newton_step = newton_step + alpha * direction
        residual = residual - alpha * image
        if iteration + 1 < ITERS:
            precond = precondition(residual)
            inner_next = jnp.sum(residual * precond)
            direction = precond + inner_next / inner_now * direction
            inner_now = inner_next
    return (newton_step, residual)
```

```python
import math

import jax
import jax.numpy as jnp
from jax import lax
from jax.sharding import PartitionSpec as P

damping = 0.3


def product(left, right):
    return jnp.dot(left, right, preferred_element_type=jnp.float32)


def transposed_term(matrix, right):
    return lax.dot_general(
        matrix, right, (((0,), (0,)), ((), ())), preferred_element_type=jnp.float32
    )


def body(activations, out_grads, token_ids, forget_mask, importance, in_inverse, out_inverse):
    low = jnp.bfloat16
    tok_rows = activations.shape[0]
    total = tok_rows * lax.axis_size("fsdp")
    columns = out_inverse.shape[1]
    own = lax.axis_index("fac") * columns

    def rows_sum(partial):
        return lax.psum_scatter(partial, "fsdp", scatter_dimension=0, tiled=True)

    def all_rows(block):
        return lax.all_gather(block, "fsdp", axis=0, tiled=True)

    def all_columns(block):
        return lax.all_gather(block, "fac", axis=1, tiled=True)

    in_block = lax.dynamic_slice(in_inverse, (0, own), (in_inverse.shape[0], columns))
    in_columns = all_rows(in_block)

    keep = 1.0 - forget_mask.astype(jnp.float32)
    weights = importance[token_ids] * keep / total
    forget_grads = out_grads * forget_mask.astype(low)[:, None]
    grad_scale = 1.0 / math.sqrt(total)
    gradient_low = rows_sum((transposed_term(activations, forget_grads) * grad_scale).astype(low))

    tok_out = product(activations, in_columns)
    scaled = (tok_out * weights[:, None]).astype(low)
    both_block = rows_sum(transposed_term(activations, scaled).astype(low)).astype(jnp.float32)
    both_block = (both_block + damping * in_block.astype(jnp.float32)).astype(low)
    both = all_columns(both_block)

    def mix(matrix_low):
        return all_rows(product(all_columns(matrix_low), out_inverse).astype(low))

    start_low = -gradient_low
    start = start_low.astype(jnp.float32)
    mixed = mix(start_low)
    image_0 = product(both, mixed)
    precond_0 = product(in_inverse, mixed)
    mixed = mix(image_0.astype(low))
    precond_1 = product(in_inverse, mixed)
    image_1 = product(both, mixed)

    pairs = (
        (start, precond_0),
        (precond_0, image_0),
        (start, precond_1),
        (image_0, precond_1),
        (precond_0, image_1),
        (precond_1, image_1),
    )
    sums = lax.psum(jnp.stack([jnp.sum(a * b) for a, b in pairs]), ("fsdp", "fac"))
    return finish(start, precond_0, image_0, precond_1, image_1, sums)


def finish(start, precond_0, image_0, precond_1, image_1, sums):
    rz, energy, rq, wq, zv, qv = [sums[i] for i in range(6)]
    alpha = rz / energy
    rz_new = rz - alpha * (energy + rq) + alpha * alpha * wq
    grow = 1.0 + rz_new / rz
    energy_new = grow * grow * energy - grow * alpha * (zv + wq) + alpha * alpha * qv
    alpha_new = rz_new / energy_new
    first = alpha + alpha_new * grow
    second = alpha * alpha_new
    newton_step = first * precond_0 - second * precond_1
    residual = start - first * image_0 + second * image_1
    return newton_step, residual


def solution(mesh):
    placed = (
        P("fsdp", None),
        P("fsdp", "fac"),
        P("fsdp"),
        P("fsdp"),
        P(),
        P("fsdp", None),
        P(None, "fac"),
    )
    return jax.shard_map(
        body,
        mesh=mesh,
        in_specs=placed,
        out_specs=(P("fsdp", "fac"), P("fsdp", "fac")),
        check_vma=False,
    )
```

```python
import functools
import math

import jax
import jax.numpy as jnp
from jax import lax
from jax.experimental import pallas as pl
from jax.experimental.pallas import tpu as pltpu
from jax.sharding import PartitionSpec as P

damping = 0.3
MESH = pl.DeviceIdType.MESH
VMEM_BYTES = 40 * 1024 * 1024


def product(left, right):
    return jnp.dot(left, right, preferred_element_type=jnp.float32)


def transposed_term(matrix, right):
    return lax.dot_general(
        matrix, right, (((0,), (0,)), ((), ())), preferred_element_type=jnp.float32
    )


def index_at(place, n):
    odd = place // (n // 2)
    return 2 * (place + odd * (n - 1 - 2 * place)) + odd


def ring(n):
    me = lax.axis_index("fsdp")
    pair = me // 2
    place = pair + (me % 2) * (n - 1 - 2 * pair)
    return me, place, index_at((place + 1) % n, n), index_at((place + n - 1) % n, n)


def greet(neighbours):
    barrier = pltpu.get_barrier_semaphore()
    for neighbour in neighbours:
        pl.semaphore_signal(barrier, inc=1, device_id=neighbour, device_id_type=MESH)
    pl.semaphore_wait(barrier, len(neighbours))


def gather_kernel(n, lefts, *refs):
    left_refs, block_ref = refs[:lefts], refs[lefts]
    full_ref, product_refs = refs[lefts + 1], refs[lefts + 2 : 2 * lefts + 2]
    send_sem, recv_sem = refs[2 * lefts + 2 :]
    rows, columns = block_ref.shape
    half, piece = columns // 2, rows // 2
    me, place, following, preceding = ring(n)
    greet(({"fsdp": following}, {"fsdp": preceding}))

    full_ref[pl.ds(pl.multiple_of(me * rows, rows), rows), :] = block_ref[...]

    def owner_at(step, way):
        return index_at((place + n - step) % n if way == 0 else (place + step) % n, n)

    def copy(step, way, part):
        at = full_ref.at[
            pl.ds(pl.multiple_of(owner_at(step, way) * rows + part * piece, piece), piece),
            pl.ds(way * half, half),
        ]
        return pltpu.make_async_remote_copy(
            src_ref=at,
            dst_ref=at,
            send_sem=send_sem.at[step, way, part],
            recv_sem=recv_sem.at[step, way, part],
            device_id={"fsdp": following if way == 0 else preceding},
            device_id_type=MESH,
        )

    for way in range(2):
        for part in range(2):
            copy(0, way, part).start()
    for ref in product_refs:
        ref[...] = jnp.zeros_like(ref)

    def step_body(step, carry):
        for way in range(2):
            for part in range(2):

                @pl.when(step > 0)
                def _():
                    copy(step - 1, way, part).wait_recv()

                @pl.when((step > 0) & (step < n - 1))
                def _():
                    copy(step, way, part).start()

        for way in range(2):
            at = pl.ds(pl.multiple_of(owner_at(step, way) * rows, rows), rows)
            block = full_ref[at, way * half : (way + 1) * half]
            for left_ref, ref in zip(left_refs, product_refs):
                ref[:, way * half : (way + 1) * half] += product(left_ref[:, at], block)
        return carry

    lax.fori_loop(0, n, step_body, 0)

    def settle(step, carry):
        for way in range(2):
            for part in range(2):
                copy(step, way, part).wait_send()
        return carry

    lax.fori_loop(0, n - 1, settle, 0)


def gather_products(lefts, block, number):
    n = lax.axis_size("fsdp")
    rows, columns = block.shape
    vmem = pl.BlockSpec(memory_space=pltpu.VMEM)
    outs = [jax.ShapeDtypeStruct((n * rows, columns), block.dtype)]
    outs += [jax.ShapeDtypeStruct((left.shape[0], columns), jnp.float32) for left in lefts]
    return pl.pallas_call(
        functools.partial(gather_kernel, n, len(lefts)),
        out_shape=outs,
        in_specs=[vmem] * (len(lefts) + 1),
        out_specs=[vmem] * len(outs),
        scratch_shapes=[pltpu.SemaphoreType.DMA((n - 1, 2, 2))] * 2,
        compiler_params=pltpu.CompilerParams(
            collective_id=number, has_side_effects=True, vmem_limit_bytes=VMEM_BYTES
        ),
        cost_estimate=pl.CostEstimate(
            flops=2 * n * rows * columns * sum(left.shape[0] for left in lefts),
            bytes_accessed=2 * n * rows * columns * 8,
            transcendentals=0,
        ),
    )(*lefts, block)


def scatter_kernel(n, factor, left_ref, right_ref, out_ref, own, sent, held, send_sem, recv_sem):
    rows, columns = out_ref.shape
    half, piece = columns // 2, rows // 2
    me, place, following, preceding = ring(n)
    greet(({"fsdp": following}, {"fsdp": preceding}))

    def copy(step, way, part):
        return pltpu.make_async_remote_copy(
            src_ref=sent.at[step, way, part],
            dst_ref=held.at[step, way, part],
            send_sem=send_sem.at[step, way, part],
            recv_sem=recv_sem.at[step, way, part],
            device_id={"fsdp": following if way == 0 else preceding},
            device_id_type=MESH,
        )

    def step_body(step, carry):
        for way in range(2):
            target = index_at((place + 2 * n - 1 - step) % n if way == 0 else (place + 1 + step) % n, n)
            at = pl.ds(pl.multiple_of(target * rows, rows), rows)
            own[way] = transposed_term(left_ref[:, at], right_ref[:, way * half : (way + 1) * half])
        for part in range(2):
            for way in range(2):
                lines = slice(part * piece, (part + 1) * piece)

                @pl.when(step == 0)
                def _():
                    sent[step, way, part] = (own[way, lines, :] * factor).astype(sent.dtype)

                @pl.when(step > 0)
                def _():
                    copy(step - 1, way, part).wait_recv()
                    term = held[step - 1, way, part].astype(jnp.float32)
                    term = term + own[way, lines, :] * factor

                    @pl.when(step < n - 1)
                    def _():
                        sent[step, way, part] = term.astype(sent.dtype)

                    @pl.when(step == n - 1)
                    def _():
                        out_ref[lines, way * half : (way + 1) * half] = term

                @pl.when(step < n - 1)
                def _():
                    copy(step, way, part).start()

        return carry

    lax.fori_loop(0, n, step_body, 0)

    def settle(step, carry):
        for way in range(2):
            for part in range(2):
                copy(step, way, part).wait_send()
        return carry

    lax.fori_loop(0, n - 1, settle, 0)


def scatter_term(left, right, factor, number):
    n = lax.axis_size("fsdp")
    rows, columns = left.shape[1] // n, right.shape[1]
    vmem = pl.BlockSpec(memory_space=pltpu.VMEM)
    slots = pltpu.VMEM((n - 1, 2, 2, rows // 2, columns // 2), jnp.bfloat16)
    return pl.pallas_call(
        functools.partial(scatter_kernel, n, factor),
        out_shape=jax.ShapeDtypeStruct((rows, columns), jnp.float32),
        in_specs=[vmem] * 2,
        out_specs=vmem,
        scratch_shapes=[
            pltpu.VMEM((2, rows, columns // 2), jnp.float32),
            slots,
            slots,
            pltpu.SemaphoreType.DMA((n - 1, 2, 2)),
            pltpu.SemaphoreType.DMA((n - 1, 2, 2)),
        ],
        compiler_params=pltpu.CompilerParams(
            collective_id=number, has_side_effects=True, vmem_limit_bytes=VMEM_BYTES
        ),
        cost_estimate=pl.CostEstimate(
            flops=2 * left.shape[0] * left.shape[1] * columns,
            bytes_accessed=2 * n * rows * columns * 8,
            transcendentals=0,
        ),
    )(left, right)


def sum_kernel(sizes, own_ref, out_ref, sent, held, send_sem, recv_sem):
    stages = []
    for axis, size in sizes:
        me = lax.axis_index(axis)
        bit = 1
        while bit < size:
            stages.append({axis: me + bit * (1 - 2 * ((me // bit) % 2))})
            bit *= 2
    greet(stages)
    total = own_ref[...]
    for number, partner in enumerate(stages):
        sent[number] = total
        copy = pltpu.make_async_remote_copy(
            src_ref=sent.at[number],
            dst_ref=held.at[number],
            send_sem=send_sem.at[number],
            recv_sem=recv_sem.at[number],
            device_id=partner,
            device_id_type=MESH,
        )
        copy.start()
        copy.wait()
        total = total + held[number]
    out_ref[...] = total


def sum_everywhere(values, number):
    sizes = [(axis, lax.axis_size(axis)) for axis in ("fac", "fsdp")]
    if any(size & (size - 1) for _, size in sizes):
        return lax.psum(values, ("fsdp", "fac"))
    stages = sum(size.bit_length() - 1 for _, size in sizes)
    vmem = pl.BlockSpec(memory_space=pltpu.VMEM)
    return pl.pallas_call(
        functools.partial(sum_kernel, sizes),
        out_shape=jax.ShapeDtypeStruct(values.shape, values.dtype),
        in_specs=[vmem],
        out_specs=vmem,
        scratch_shapes=[
            pltpu.VMEM((stages, *values.shape), values.dtype),
            pltpu.VMEM((stages, *values.shape), values.dtype),
            pltpu.SemaphoreType.DMA((stages,)),
            pltpu.SemaphoreType.DMA((stages,)),
        ],
        compiler_params=pltpu.CompilerParams(collective_id=number, has_side_effects=True),
    )(values)


def body(activations, out_grads, token_ids, forget_mask, importance, in_inverse, out_inverse):
    low = jnp.bfloat16
    tok_rows = activations.shape[0]
    total = tok_rows * lax.axis_size("fsdp")
    columns = out_inverse.shape[1]
    own = lax.axis_index("fac") * columns

    shards = lax.axis_size("fsdp")
    rows = in_inverse.shape[0]
    ringed = shards % 2 == 0 and rows % 128 == 0 and columns % 256 == 0

    def rows_sum(right, factor, number):
        if ringed:
            return scatter_term(activations, right, factor, number)
        partial = (transposed_term(activations, right) * factor).astype(low)
        partial = lax.psum_scatter(partial, "fsdp", scatter_dimension=0, tiled=True)
        return partial.astype(jnp.float32)

    def all_rows(block):
        return lax.all_gather(block, "fsdp", axis=0, tiled=True)

    def all_columns(block):
        return lax.all_gather(block, "fac", axis=1, tiled=True)

    in_block = lax.dynamic_slice(in_inverse, (0, own), (in_inverse.shape[0], columns))
    in_columns = all_rows(in_block)

    keep = 1.0 - forget_mask.astype(jnp.float32)
    weights = importance[token_ids] * keep / total
    forget_grads = out_grads * forget_mask.astype(low)[:, None]
    grad_scale = 1.0 / math.sqrt(total)
    start = -rows_sum(forget_grads, grad_scale, 0)

    tok_out = product(activations, in_columns)
    scaled = (tok_out * weights[:, None]).astype(low)
    both_block = rows_sum(scaled, 1.0, 1)
    both_block = (both_block + damping * in_block.astype(jnp.float32)).astype(low)
    both = all_columns(both_block)

    def mix(matrix):
        return product(all_columns(matrix.astype(low)), out_inverse).astype(low)

    mixed = mix(start)
    if ringed:
        mixed, precond_0 = gather_products((in_inverse,), mixed, 2)
    else:
        mixed = all_rows(mixed)
        precond_0 = product(in_inverse, mixed)
    image_0 = product(both, mixed)
    mixed = mix(image_0)
    if ringed:
        _, precond_1, image_1 = gather_products((in_inverse, both), mixed, 3)
    else:
        mixed = all_rows(mixed)
        precond_1 = product(in_inverse, mixed)
        image_1 = product(both, mixed)

    pairs = (
        (start, precond_0),
        (precond_0, image_0),
        (start, precond_1),
        (image_0, precond_1),
        (precond_0, image_1),
        (precond_1, image_1),
    )
    lane = lax.broadcasted_iota(jnp.int32, (8, 128), 1)
    local = jnp.zeros((8, 128), jnp.float32)
    for number, (left, right) in enumerate(pairs):
        local = jnp.where(lane == number, jnp.sum(left * right), local)
    sums = sum_everywhere(local, 4)[0]
    return finish(start, precond_0, image_0, precond_1, image_1, sums)


def finish(start, precond_0, image_0, precond_1, image_1, sums):
    rz, energy, rq, wq, zv, qv = [sums[i] for i in range(6)]
    alpha = rz / energy
    rz_new = rz - alpha * (energy + rq) + alpha * alpha * wq
    grow = 1.0 + rz_new / rz
    energy_new = grow * grow * energy - grow * alpha * (zv + wq) + alpha * alpha * qv
    alpha_new = rz_new / energy_new
    first = alpha + alpha_new * grow
    second = alpha * alpha_new
    newton_step = first * precond_0 - second * precond_1
    residual = start - first * image_0 + second * image_1
    return newton_step, residual


def solution(mesh):
    placed = (
        P("fsdp", None),
        P("fsdp", "fac"),
        P("fsdp"),
        P("fsdp"),
        P(),
        P("fsdp", None),
        P(None, "fac"),
    )
    return jax.shard_map(
        body,
        mesh=mesh,
        in_specs=placed,
        out_specs=(P("fsdp", "fac"), P("fsdp", "fac")),
        check_vma=False,
    )
```

```python
import functools
import math

import jax
import jax.numpy as jnp
from jax import lax
from jax.experimental import pallas as pl
from jax.experimental.pallas import tpu as pltpu
from jax.sharding import PartitionSpec as P

damping = 0.3
MESH = pl.DeviceIdType.MESH
VMEM_BYTES = 40 * 1024 * 1024


def product(left, right):
    return jnp.dot(left, right, preferred_element_type=jnp.float32)


def transposed_term(matrix, right):
    return lax.dot_general(
        matrix, right, (((0,), (0,)), ((), ())), preferred_element_type=jnp.float32
    )


def index_at(place, n):
    odd = place // (n // 2)
    return 2 * (place + odd * (n - 1 - 2 * place)) + odd


def ring(n):
    me = lax.axis_index("fsdp")
    pair = me // 2
    place = pair + (me % 2) * (n - 1 - 2 * pair)
    return me, place, index_at((place + 1) % n, n), index_at((place + n - 1) % n, n)


def greet(neighbours):
    barrier = pltpu.get_barrier_semaphore()
    for neighbour in neighbours:
        pl.semaphore_signal(barrier, inc=1, device_id=neighbour, device_id_type=MESH)
    pl.semaphore_wait(barrier, len(neighbours))


def gather_kernel(n, lefts, *refs):
    left_refs, block_ref = refs[:lefts], refs[lefts]
    full_ref, product_refs = refs[lefts + 1], refs[lefts + 2 : 2 * lefts + 2]
    send_sem, recv_sem = refs[2 * lefts + 2 :]
    rows, columns = block_ref.shape
    half, piece = columns // 2, rows // 2
    me, place, following, preceding = ring(n)
    greet(({"fsdp": following}, {"fsdp": preceding}))

    full_ref[pl.ds(pl.multiple_of(me * rows, rows), rows), :] = block_ref[...]

    def owner_at(step, way):
        return index_at((place + n - step) % n if way == 0 else (place + step) % n, n)

    def copy(step, way, part):
        at = full_ref.at[
            pl.ds(pl.multiple_of(owner_at(step, way) * rows + part * piece, piece), piece),
            pl.ds(way * half, half),
        ]
        return pltpu.make_async_remote_copy(
            src_ref=at,
            dst_ref=at,
            send_sem=send_sem.at[step, way, part],
            recv_sem=recv_sem.at[step, way, part],
            device_id={"fsdp": following if way == 0 else preceding},
            device_id_type=MESH,
        )

    for way in range(2):
        for part in range(2):
            copy(0, way, part).start()
    for ref in product_refs:
        ref[...] = jnp.zeros_like(ref)

    def step_body(step, carry):
        for way in range(2):
            for part in range(2):

                @pl.when(step > 0)
                def _():
                    copy(step - 1, way, part).wait_recv()

                @pl.when((step > 0) & (step < n - 1))
                def _():
                    copy(step, way, part).start()

        for way in range(2):
            at = pl.ds(pl.multiple_of(owner_at(step, way) * rows, rows), rows)
            block = full_ref[at, way * half : (way + 1) * half]
            for left_ref, ref in zip(left_refs, product_refs):
                ref[:, way * half : (way + 1) * half] += product(left_ref[:, at], block)
        return carry

    lax.fori_loop(0, n, step_body, 0)

    def settle(step, carry):
        for way in range(2):
            for part in range(2):
                copy(step, way, part).wait_send()
        return carry

    lax.fori_loop(0, n - 1, settle, 0)


def gather_products(lefts, block, number):
    n = lax.axis_size("fsdp")
    rows, columns = block.shape
    vmem = pl.BlockSpec(memory_space=pltpu.VMEM)
    outs = [jax.ShapeDtypeStruct((n * rows, columns), block.dtype)]
    outs += [jax.ShapeDtypeStruct((left.shape[0], columns), jnp.float32) for left in lefts]
    return pl.pallas_call(
        functools.partial(gather_kernel, n, len(lefts)),
        out_shape=outs,
        in_specs=[vmem] * (len(lefts) + 1),
        out_specs=[vmem] * len(outs),
        scratch_shapes=[pltpu.SemaphoreType.DMA((n - 1, 2, 2))] * 2,
        compiler_params=pltpu.CompilerParams(
            collective_id=number, has_side_effects=True, vmem_limit_bytes=VMEM_BYTES
        ),
        cost_estimate=pl.CostEstimate(
            flops=2 * n * rows * columns * sum(left.shape[0] for left in lefts),
            bytes_accessed=2 * n * rows * columns * 8,
            transcendentals=0,
        ),
    )(*lefts, block)


def scatter_kernel(n, factor, left_ref, right_ref, out_ref, own, sent, held, send_sem, recv_sem):
    rows, columns = out_ref.shape
    half, piece = columns // 2, rows // 2
    me, place, following, preceding = ring(n)
    greet(({"fsdp": following}, {"fsdp": preceding}))

    def copy(step, way, part):
        return pltpu.make_async_remote_copy(
            src_ref=sent.at[step, way, part],
            dst_ref=held.at[step, way, part],
            send_sem=send_sem.at[step, way, part],
            recv_sem=recv_sem.at[step, way, part],
            device_id={"fsdp": following if way == 0 else preceding},
            device_id_type=MESH,
        )

    def step_body(step, carry):
        for way in range(2):
            target = index_at((place + 2 * n - 1 - step) % n if way == 0 else (place + 1 + step) % n, n)
            at = pl.ds(pl.multiple_of(target * rows, rows), rows)
            own[way] = transposed_term(left_ref[:, at], right_ref[:, way * half : (way + 1) * half])
        for part in range(2):
            for way in range(2):
                lines = slice(part * piece, (part + 1) * piece)

                @pl.when(step == 0)
                def _():
                    sent[step, way, part] = (own[way, lines, :] * factor).astype(sent.dtype)

                @pl.when(step > 0)
                def _():
                    copy(step - 1, way, part).wait_recv()
                    term = held[step - 1, way, part].astype(jnp.float32)
                    term = term + own[way, lines, :] * factor

                    @pl.when(step < n - 1)
                    def _():
                        sent[step, way, part] = term.astype(sent.dtype)

                    @pl.when(step == n - 1)
                    def _():
                        out_ref[lines, way * half : (way + 1) * half] = term

                @pl.when(step < n - 1)
                def _():
                    copy(step, way, part).start()

        return carry

    lax.fori_loop(0, n, step_body, 0)

    def settle(step, carry):
        for way in range(2):
            for part in range(2):
                copy(step, way, part).wait_send()
        return carry

    lax.fori_loop(0, n - 1, settle, 0)


def scatter_term(left, right, factor, number):
    n = lax.axis_size("fsdp")
    rows, columns = left.shape[1] // n, right.shape[1]
    vmem = pl.BlockSpec(memory_space=pltpu.VMEM)
    slots = pltpu.VMEM((n - 1, 2, 2, rows // 2, columns // 2), jnp.bfloat16)
    return pl.pallas_call(
        functools.partial(scatter_kernel, n, factor),
        out_shape=jax.ShapeDtypeStruct((rows, columns), jnp.float32),
        in_specs=[vmem] * 2,
        out_specs=vmem,
        scratch_shapes=[
            pltpu.VMEM((2, rows, columns // 2), jnp.float32),
            slots,
            slots,
            pltpu.SemaphoreType.DMA((n - 1, 2, 2)),
            pltpu.SemaphoreType.DMA((n - 1, 2, 2)),
        ],
        compiler_params=pltpu.CompilerParams(
            collective_id=number, has_side_effects=True, vmem_limit_bytes=VMEM_BYTES
        ),
        cost_estimate=pl.CostEstimate(
            flops=2 * left.shape[0] * left.shape[1] * columns,
            bytes_accessed=2 * n * rows * columns * 8,
            transcendentals=0,
        ),
    )(left, right)


def spread_kernel(both_ref, mixed_ref, right_ref, image_ref, out_ref, held, send_sem, recv_sem):
    rows, columns = image_ref.shape
    piece = rows // 2
    me = lax.axis_index("fac")
    beside = {"fac": me + 1 - 2 * (me % 2)}
    across = {"fac": (me + 2) % 4}
    greet((beside, across))

    def copy(number, part):
        source, slot, to = ((0, 1, beside), (0, 2, across), (2, 3, beside))[number]
        return pltpu.make_async_remote_copy(
            src_ref=held.at[source, part],
            dst_ref=held.at[slot, part],
            send_sem=send_sem.at[number, part],
            recv_sem=recv_sem.at[number, part],
            device_id=to,
            device_id_type=MESH,
        )

    def add(slot, owner):
        at = pl.ds(pl.multiple_of(owner * columns, columns), columns)
        for part in range(2):
            term = product(held[slot, part], right_ref[at, :])
            lines = slice(part * piece, (part + 1) * piece)
            image = term if slot == 0 else term + total[part]
            total[part] = image
            if slot == 3:
                out_ref[lines, :] = image.astype(out_ref.dtype)

    total = [None, None]
    for part in range(2):
        lines = slice(part * piece, (part + 1) * piece)
        image_ref[lines, :] = product(both_ref[lines, :], mixed_ref[...])
        held[0, part] = image_ref[lines, :].astype(held.dtype)
        copy(1, part).start()
        copy(0, part).start()
    add(0, me)
    for part in range(2):
        copy(0, part).wait_recv()
    add(1, me + 1 - 2 * (me % 2))
    for part in range(2):
        copy(1, part).wait_recv()
        copy(2, part).start()
    add(2, (me + 2) % 4)
    for part in range(2):
        copy(2, part).wait_recv()
    add(3, (me + 1 - 2 * (me % 2) + 2) % 4)
    for number in range(3):
        for part in range(2):
            copy(number, part).wait_send()


def spread(both, mixed, right, number):
    rows, columns = both.shape[0], mixed.shape[1]
    vmem = pl.BlockSpec(memory_space=pltpu.VMEM)
    return pl.pallas_call(
        spread_kernel,
        out_shape=(
            jax.ShapeDtypeStruct((rows, columns), jnp.float32),
            jax.ShapeDtypeStruct((rows, columns), jnp.bfloat16),
        ),
        in_specs=[vmem] * 3,
        out_specs=(vmem, vmem),
        scratch_shapes=[
            pltpu.VMEM((4, 2, rows // 2, columns), jnp.bfloat16),
            pltpu.SemaphoreType.DMA((3, 2)),
            pltpu.SemaphoreType.DMA((3, 2)),
        ],
        compiler_params=pltpu.CompilerParams(
            collective_id=number, has_side_effects=True, vmem_limit_bytes=VMEM_BYTES
        ),
        cost_estimate=pl.CostEstimate(
            flops=2 * rows * columns * (both.shape[1] + right.shape[0]),
            bytes_accessed=2 * (mixed.size + right.size),
            transcendentals=0,
        ),
    )(both, mixed, right)


PAIRS = ((0, 1), (1, 2), (0, 3), (2, 3), (1, 4), (3, 4))


def finish_kernel(sizes, *refs):
    blocks, outs = refs[:5], refs[5:7]
    sent, held, send_sem, recv_sem = refs[7:]
    rows, columns = outs[0].shape

    stages = []
    for axis, size in sizes:
        me = lax.axis_index(axis)
        stages.append([{axis: (me + away) % size} for away in range(1, size)])
    greet(stages[0] + stages[1])

    def lines_at(row):
        return pl.ds(pl.multiple_of(row * 8, 8), 8)

    def add_row(row, sums):
        values = [ref[lines_at(row), :] for ref in blocks]
        return tuple(total + values[a] * values[b] for total, (a, b) in zip(sums, PAIRS))

    sums = lax.fori_loop(0, rows // 8, add_row, (jnp.zeros((8, columns), jnp.float32),) * len(PAIRS))
    sums = [sum(one[:, lane : lane + 128] for lane in range(0, columns, 128)) for one in sums]
    slot = 0
    for stage, peers in enumerate(stages):
        for number, one in enumerate(sums):
            sent[stage, number] = one
        copies = []
        for peer in peers:
            copies.append(
                pltpu.make_async_remote_copy(
                    src_ref=sent.at[stage],
                    dst_ref=held.at[slot],
                    send_sem=send_sem.at[slot],
                    recv_sem=recv_sem.at[slot],
                    device_id=peer,
                    device_id_type=MESH,
                )
            )
            copies[-1].start()
            slot += 1
        for place, one in enumerate(copies):
            one.wait()
            at = slot - len(copies) + place
            sums = [total + held[at, number] for number, total in enumerate(sums)]

    rz, energy, rq, wq, zv, qv = [jnp.sum(one, axis=(0, 1), keepdims=True) for one in sums]
    alpha = rz / energy
    rz_new = rz - alpha * (energy + rq) + alpha * alpha * wq
    grow = 1.0 + rz_new / rz
    energy_new = grow * grow * energy - grow * alpha * (zv + wq) + alpha * alpha * qv
    alpha_new = rz_new / energy_new
    first = jnp.broadcast_to(alpha + alpha_new * grow, (8, columns))
    second = jnp.broadcast_to(alpha * alpha_new, (8, columns))

    def write_row(row, carry):
        at = lines_at(row)
        start, precond_0, image_0, precond_1, image_1 = [ref[at, :] for ref in blocks]
        outs[0][at, :] = first * precond_0 - second * precond_1
        outs[1][at, :] = start - first * image_0 + second * image_1
        return carry

    lax.fori_loop(0, rows // 8, write_row, 0)


def finish(blocks, number):
    sizes = [(axis, lax.axis_size(axis)) for axis in ("fac", "fsdp")]
    peers = sum(size - 1 for _, size in sizes)
    vmem = pl.BlockSpec(memory_space=pltpu.VMEM)
    shape = jax.ShapeDtypeStruct(blocks[0].shape, jnp.float32)
    return pl.pallas_call(
        functools.partial(finish_kernel, sizes),
        out_shape=(shape, shape),
        in_specs=[vmem] * 5,
        out_specs=(vmem, vmem),
        scratch_shapes=[
            pltpu.VMEM((2, len(PAIRS), 8, 128), jnp.float32),
            pltpu.VMEM((peers, len(PAIRS), 8, 128), jnp.float32),
            pltpu.SemaphoreType.DMA((peers,)),
            pltpu.SemaphoreType.DMA((peers,)),
        ],
        compiler_params=pltpu.CompilerParams(
            collective_id=number, has_side_effects=True, vmem_limit_bytes=VMEM_BYTES
        ),
    )(*blocks)


def body(activations, out_grads, token_ids, forget_mask, importance, in_inverse, out_inverse):
    low = jnp.bfloat16
    tok_rows = activations.shape[0]
    total = tok_rows * lax.axis_size("fsdp")
    columns = out_inverse.shape[1]
    own = lax.axis_index("fac") * columns

    shards = lax.axis_size("fsdp")
    rows = in_inverse.shape[0]
    ringed = shards % 2 == 0 and rows % 128 == 0 and columns % 256 == 0

    def rows_sum(right, factor, number):
        if ringed:
            return scatter_term(activations, right, factor, number)
        partial = (transposed_term(activations, right) * factor).astype(low)
        partial = lax.psum_scatter(partial, "fsdp", scatter_dimension=0, tiled=True)
        return partial.astype(jnp.float32)

    def all_rows(block):
        return lax.all_gather(block, "fsdp", axis=0, tiled=True)

    def all_columns(block):
        return lax.all_gather(block, "fac", axis=1, tiled=True)

    in_block = lax.dynamic_slice(in_inverse, (0, own), (in_inverse.shape[0], columns))
    if ringed:
        _, tok_out = gather_products((activations,), in_block, 0)
    else:
        tok_out = product(activations, all_rows(in_block))

    keep = 1.0 - forget_mask.astype(jnp.float32)
    weights = importance[token_ids] * keep / total
    forget_grads = out_grads * forget_mask.astype(low)[:, None]
    grad_scale = 1.0 / math.sqrt(total)
    scaled = (tok_out * weights[:, None]).astype(low)
    forget_grads, scaled = lax.optimization_barrier((forget_grads, scaled))
    start = -rows_sum(forget_grads, grad_scale, 1)
    start, scaled = lax.optimization_barrier((start, scaled))
    both_block = rows_sum(scaled, 1.0, 2)
    both_block = (both_block + damping * in_block.astype(jnp.float32)).astype(low)
    both = all_columns(both_block)

    def mix(matrix):
        return product(all_columns(matrix.astype(low)), out_inverse).astype(low)

    mixed = mix(start)
    if ringed:
        mixed, precond_0 = gather_products((in_inverse,), mixed, 3)
    else:
        mixed = all_rows(mixed)
        precond_0 = product(in_inverse, mixed)
    if ringed and lax.axis_size("fac") == 4:
        image_0, mixed = spread(both, mixed, out_inverse, 4)
    else:
        image_0 = product(both, mixed)
        mixed = mix(image_0)
    if ringed:
        _, precond_1, image_1 = gather_products((in_inverse, both), mixed, 5)
    else:
        mixed = all_rows(mixed)
        precond_1 = product(in_inverse, mixed)
        image_1 = product(both, mixed)

    return finish((start, precond_0, image_0, precond_1, image_1), 6)


def solution(mesh):
    placed = (
        P("fsdp", None),
        P("fsdp", "fac"),
        P("fsdp"),
        P("fsdp"),
        P(),
        P("fsdp", None),
        P(None, "fac"),
    )
    return jax.shard_map(
        body,
        mesh=mesh,
        in_specs=placed,
        out_specs=(P("fsdp", "fac"), P("fsdp", "fac")),
        check_vma=False,
    )
```

```python
import functools
import math

import jax
import jax.numpy as jnp
from jax import lax
from jax.experimental import pallas as pl
from jax.experimental.pallas import tpu as pltpu
from jax.sharding import PartitionSpec as P

damping = 0.3
MESH = pl.DeviceIdType.MESH
VMEM_BYTES = 24 * 1024 * 1024


def product(left, right):
    return jnp.dot(left, right, preferred_element_type=jnp.float32)


def transposed_term(matrix, right):
    return lax.dot_general(
        matrix, right, (((0,), (0,)), ((), ())), preferred_element_type=jnp.float32
    )


def index_at(place, n):
    odd = place // (n // 2)
    return 2 * (place + odd * (n - 1 - 2 * place)) + odd


def ring(n):
    me = lax.axis_index("fsdp")
    pair = me // 2
    place = pair + (me % 2) * (n - 1 - 2 * pair)
    return me, place, index_at((place + 1) % n, n), index_at((place + n - 1) % n, n)


def greet(neighbours):
    barrier = pltpu.get_barrier_semaphore()
    for neighbour in neighbours:
        pl.semaphore_signal(barrier, inc=1, device_id=neighbour, device_id_type=MESH)
    pl.semaphore_wait(barrier, len(neighbours))


def gather_kernel(n, lefts, mixing, *refs):
    left_refs, block_ref, refs = refs[:lefts], refs[lefts], refs[lefts + 1 :]
    if mixing:
        right_ref, refs = refs[0], refs[1:]
    product_refs, full_ref = refs[:lefts], refs[lefts]
    send_sem, recv_sem = refs[lefts + 1 :]
    rows, columns = full_ref.shape[0] // n, full_ref.shape[1]
    half, piece = columns // 2, rows // 2
    me, place, following, preceding = ring(n)
    greet(({"fsdp": following}, {"fsdp": preceding}))

    def owner_at(step, way):
        return index_at((place + n - step) % n if way == 0 else (place + step) % n, n)

    def copy(step, way, part):
        at = full_ref.at[
            pl.ds(pl.multiple_of(owner_at(step, way) * rows + part * piece, piece), piece),
            pl.ds(way * half, half),
        ]
        return pltpu.make_async_remote_copy(
            src_ref=at,
            dst_ref=at,
            send_sem=send_sem.at[step, way, part],
            recv_sem=recv_sem.at[step, way, part],
            device_id={"fsdp": following if way == 0 else preceding},
            device_id_type=MESH,
        )

    for part in range(2):
        for way in range(2):
            lines, lanes = slice(part * piece, (part + 1) * piece), slice(way * half, (way + 1) * half)
            if mixing:
                block = product(block_ref[lines, :], right_ref[:, lanes]).astype(full_ref.dtype)
            else:
                block = block_ref[lines, lanes]
            full_ref[pl.ds(pl.multiple_of(me * rows + part * piece, piece), piece), lanes] = block
            copy(0, way, part).start()
    for ref in product_refs:
        ref[...] = jnp.zeros_like(ref)

    def step_body(step, carry):
        for way in range(2):
            for part in range(2):

                @pl.when(step > 0)
                def _():
                    copy(step - 1, way, part).wait_recv()

                @pl.when((step > 0) & (step < n - 1))
                def _():
                    copy(step, way, part).start()

        for way in range(2):
            at = pl.ds(pl.multiple_of(owner_at(step, way) * rows, rows), rows)
            block = full_ref[at, way * half : (way + 1) * half]
            for left_ref, ref in zip(left_refs, product_refs):
                ref[:, way * half : (way + 1) * half] += product(left_ref[:, at], block)
        return carry

    lax.fori_loop(0, n, step_body, 0)

    def settle(step, carry):
        for way in range(2):
            for part in range(2):
                copy(step, way, part).wait_send()
        return carry

    lax.fori_loop(0, n - 1, settle, 0)


def gather_products(lefts, block, number, right=None, keep=False):
    n = lax.axis_size("fsdp")
    rows, columns = block.shape[0], (block if right is None else right).shape[1]
    operands = (*lefts, block) if right is None else (*lefts, block, right)
    vmem = pl.BlockSpec(memory_space=pltpu.VMEM)
    outs = [jax.ShapeDtypeStruct((left.shape[0], columns), jnp.float32) for left in lefts]
    scratch = [pltpu.SemaphoreType.DMA((n - 1, 2, 2))] * 2
    if keep:
        outs.append(jax.ShapeDtypeStruct((n * rows, columns), block.dtype))
    else:
        scratch.insert(0, pltpu.VMEM((n * rows, columns), block.dtype))
    return pl.pallas_call(
        functools.partial(gather_kernel, n, len(lefts), right is not None),
        out_shape=outs,
        in_specs=[vmem] * len(operands),
        out_specs=[vmem] * len(outs),
        scratch_shapes=scratch,
        compiler_params=pltpu.CompilerParams(
            collective_id=number, has_side_effects=True, vmem_limit_bytes=VMEM_BYTES
        ),
        cost_estimate=pl.CostEstimate(
            flops=2 * n * rows * columns * sum(left.shape[0] for left in lefts),
            bytes_accessed=2 * n * rows * columns * 8,
            transcendentals=0,
        ),
    )(*operands)


def scatter_kernel(n, factor, left_ref, right_ref, out_ref, own, sent, held, send_sem, recv_sem):
    rows, columns = out_ref.shape
    half, piece = columns // 2, rows // 2
    me, place, following, preceding = ring(n)
    greet(({"fsdp": following}, {"fsdp": preceding}))

    def copy(step, way, part):
        return pltpu.make_async_remote_copy(
            src_ref=sent.at[step, way, part],
            dst_ref=held.at[step, way, part],
            send_sem=send_sem.at[step, way, part],
            recv_sem=recv_sem.at[step, way, part],
            device_id={"fsdp": following if way == 0 else preceding},
            device_id_type=MESH,
        )

    def step_body(step, carry):
        for way in range(2):
            target = index_at((place + 2 * n - 1 - step) % n if way == 0 else (place + 1 + step) % n, n)
            at = pl.ds(pl.multiple_of(target * rows, rows), rows)
            own[way] = transposed_term(left_ref[:, at], right_ref[:, way * half : (way + 1) * half])
        for part in range(2):
            for way in range(2):
                lines = slice(part * piece, (part + 1) * piece)

                @pl.when(step == 0)
                def _():
                    sent[step, way, part] = (own[way, lines, :] * factor).astype(sent.dtype)

                @pl.when(step > 0)
                def _():
                    copy(step - 1, way, part).wait_recv()
                    term = held[step - 1, way, part].astype(jnp.float32)
                    term = term + own[way, lines, :] * factor

                    @pl.when(step < n - 1)
                    def _():
                        sent[step, way, part] = term.astype(sent.dtype)

                    @pl.when(step == n - 1)
                    def _():
                        out_ref[lines, way * half : (way + 1) * half] = term

                @pl.when(step < n - 1)
                def _():
                    copy(step, way, part).start()

        return carry

    lax.fori_loop(0, n, step_body, 0)

    def settle(step, carry):
        for way in range(2):
            for part in range(2):
                copy(step, way, part).wait_send()
        return carry

    lax.fori_loop(0, n - 1, settle, 0)


def scatter_term(left, right, factor, number):
    n = lax.axis_size("fsdp")
    rows, columns = left.shape[1] // n, right.shape[1]
    vmem = pl.BlockSpec(memory_space=pltpu.VMEM)
    slots = pltpu.VMEM((n - 1, 2, 2, rows // 2, columns // 2), jnp.bfloat16)
    return pl.pallas_call(
        functools.partial(scatter_kernel, n, factor),
        out_shape=jax.ShapeDtypeStruct((rows, columns), jnp.float32),
        in_specs=[vmem] * 2,
        out_specs=vmem,
        scratch_shapes=[
            pltpu.VMEM((2, rows, columns // 2), jnp.float32),
            slots,
            slots,
            pltpu.SemaphoreType.DMA((n - 1, 2, 2)),
            pltpu.SemaphoreType.DMA((n - 1, 2, 2)),
        ],
        compiler_params=pltpu.CompilerParams(
            collective_id=number, has_side_effects=True, vmem_limit_bytes=VMEM_BYTES
        ),
        cost_estimate=pl.CostEstimate(
            flops=2 * left.shape[0] * left.shape[1] * columns,
            bytes_accessed=2 * n * rows * columns * 8,
            transcendentals=0,
        ),
    )(left, right)


def spread_kernel(both_ref, mixed_ref, right_ref, image_ref, out_ref, held, send_sem, recv_sem):
    rows, columns = image_ref.shape
    piece = rows // 2
    me = lax.axis_index("fac")
    beside = {"fac": me + 1 - 2 * (me % 2)}
    across = {"fac": (me + 2) % 4}
    greet((beside, across))

    def copy(number, part):
        source, slot, to = ((0, 1, beside), (0, 2, across), (2, 3, beside))[number]
        return pltpu.make_async_remote_copy(
            src_ref=held.at[source, part],
            dst_ref=held.at[slot, part],
            send_sem=send_sem.at[number, part],
            recv_sem=recv_sem.at[number, part],
            device_id=to,
            device_id_type=MESH,
        )

    def add(slot, owner):
        at = pl.ds(pl.multiple_of(owner * columns, columns), columns)
        for part in range(2):
            term = product(held[slot, part], right_ref[at, :])
            lines = slice(part * piece, (part + 1) * piece)
            image = term if slot == 0 else term + total[part]
            total[part] = image
            if slot == 3:
                out_ref[lines, :] = image.astype(out_ref.dtype)

    total = [None, None]
    for part in range(2):
        lines = slice(part * piece, (part + 1) * piece)
        image_ref[lines, :] = product(both_ref[lines, :], mixed_ref[...])
        held[0, part] = image_ref[lines, :].astype(held.dtype)
        copy(1, part).start()
        copy(0, part).start()
    add(0, me)
    for part in range(2):
        copy(0, part).wait_recv()
    add(1, me + 1 - 2 * (me % 2))
    for part in range(2):
        copy(1, part).wait_recv()
        copy(2, part).start()
    add(2, (me + 2) % 4)
    for part in range(2):
        copy(2, part).wait_recv()
    add(3, (me + 1 - 2 * (me % 2) + 2) % 4)
    for number in range(3):
        for part in range(2):
            copy(number, part).wait_send()


def spread(both, mixed, right, number):
    rows, columns = both.shape[0], mixed.shape[1]
    vmem = pl.BlockSpec(memory_space=pltpu.VMEM)
    return pl.pallas_call(
        spread_kernel,
        out_shape=(
            jax.ShapeDtypeStruct((rows, columns), jnp.float32),
            jax.ShapeDtypeStruct((rows, columns), jnp.bfloat16),
        ),
        in_specs=[vmem] * 3,
        out_specs=(vmem, vmem),
        scratch_shapes=[
            pltpu.VMEM((4, 2, rows // 2, columns), jnp.bfloat16),
            pltpu.SemaphoreType.DMA((3, 2)),
            pltpu.SemaphoreType.DMA((3, 2)),
        ],
        compiler_params=pltpu.CompilerParams(
            collective_id=number, has_side_effects=True, vmem_limit_bytes=VMEM_BYTES
        ),
        cost_estimate=pl.CostEstimate(
            flops=2 * rows * columns * (both.shape[1] + right.shape[0]),
            bytes_accessed=2 * (mixed.size + right.size),
            transcendentals=0,
        ),
    )(both, mixed, right)


PAIRS = ((0, 1), (1, 2), (0, 3), (2, 3), (1, 4), (3, 4))


def finish_kernel(sizes, *refs):
    blocks, outs = refs[:5], refs[5:7]
    sent, held, send_sem, recv_sem = refs[7:]
    rows, columns = outs[0].shape

    stages = []
    for axis, size in sizes:
        me = lax.axis_index(axis)
        stages.append([{axis: (me + away) % size} for away in range(1, size)])
    greet(stages[0] + stages[1])

    def lines_at(row):
        return pl.ds(pl.multiple_of(row * 8, 8), 8)

    def add_row(row, sums):
        values = [ref[lines_at(row), :] for ref in blocks]
        return tuple(total + values[a] * values[b] for total, (a, b) in zip(sums, PAIRS))

    sums = lax.fori_loop(0, rows // 8, add_row, (jnp.zeros((8, columns), jnp.float32),) * len(PAIRS))
    sums = [sum(one[:, lane : lane + 128] for lane in range(0, columns, 128)) for one in sums]
    slot = 0
    for stage, peers in enumerate(stages):
        for number, one in enumerate(sums):
            sent[stage, number] = one
        copies = []
        for peer in peers:
            copies.append(
                pltpu.make_async_remote_copy(
                    src_ref=sent.at[stage],
                    dst_ref=held.at[slot],
                    send_sem=send_sem.at[slot],
                    recv_sem=recv_sem.at[slot],
                    device_id=peer,
                    device_id_type=MESH,
                )
            )
            copies[-1].start()
            slot += 1
        for place, one in enumerate(copies):
            one.wait()
            at = slot - len(copies) + place
            sums = [total + held[at, number] for number, total in enumerate(sums)]

    rz, energy, rq, wq, zv, qv = [jnp.sum(one, axis=(0, 1), keepdims=True) for one in sums]
    alpha = rz / energy
    rz_new = rz - alpha * (energy + rq) + alpha * alpha * wq
    grow = 1.0 + rz_new / rz
    energy_new = grow * grow * energy - grow * alpha * (zv + wq) + alpha * alpha * qv
    alpha_new = rz_new / energy_new
    first = jnp.broadcast_to(alpha + alpha_new * grow, (8, columns))
    second = jnp.broadcast_to(alpha * alpha_new, (8, columns))

    def write_row(row, carry):
        at = lines_at(row)
        start, precond_0, image_0, precond_1, image_1 = [ref[at, :] for ref in blocks]
        outs[0][at, :] = first * precond_0 - second * precond_1
        outs[1][at, :] = start - first * image_0 + second * image_1
        return carry

    lax.fori_loop(0, rows // 8, write_row, 0)


def finish(blocks, number):
    sizes = [(axis, lax.axis_size(axis)) for axis in ("fac", "fsdp")]
    peers = sum(size - 1 for _, size in sizes)
    vmem = pl.BlockSpec(memory_space=pltpu.VMEM)
    shape = jax.ShapeDtypeStruct(blocks[0].shape, jnp.float32)
    return pl.pallas_call(
        functools.partial(finish_kernel, sizes),
        out_shape=(shape, shape),
        in_specs=[vmem] * 5,
        out_specs=(vmem, vmem),
        scratch_shapes=[
            pltpu.VMEM((2, len(PAIRS), 8, 128), jnp.float32),
            pltpu.VMEM((peers, len(PAIRS), 8, 128), jnp.float32),
            pltpu.SemaphoreType.DMA((peers,)),
            pltpu.SemaphoreType.DMA((peers,)),
        ],
        compiler_params=pltpu.CompilerParams(
            collective_id=number, has_side_effects=True, vmem_limit_bytes=VMEM_BYTES
        ),
    )(*blocks)


def look_up(table, ids):
    fold = 256
    if table.shape[0] % fold:
        return table[ids]
    folded = table.reshape(-1, fold)
    row, lane = ids[:, None] // fold, ids[:, None] % fold
    chosen = (row == jnp.arange(folded.shape[0])).astype(jnp.float32)
    near = jnp.dot(chosen, folded, precision=lax.Precision.HIGHEST)
    return jnp.sum(jnp.where(lane == jnp.arange(fold), near, 0.0), axis=1)


def body(activations, out_grads, token_ids, forget_mask, importance, in_inverse, out_inverse):
    low = jnp.bfloat16
    tok_rows = activations.shape[0]
    total = tok_rows * lax.axis_size("fsdp")
    columns = out_inverse.shape[1]
    own = lax.axis_index("fac") * columns

    shards = lax.axis_size("fsdp")
    rows = in_inverse.shape[0]
    ringed = shards % 2 == 0 and rows % 128 == 0 and columns % 256 == 0

    def rows_sum(right, factor, number):
        if ringed:
            return scatter_term(activations, right, factor, number)
        partial = (transposed_term(activations, right) * factor).astype(low)
        partial = lax.psum_scatter(partial, "fsdp", scatter_dimension=0, tiled=True)
        return partial.astype(jnp.float32)

    def all_rows(block):
        return lax.all_gather(block, "fsdp", axis=0, tiled=True)

    def all_columns(block):
        return lax.all_gather(block, "fac", axis=1, tiled=True)

    in_block = lax.dynamic_slice(in_inverse, (0, own), (in_inverse.shape[0], columns))
    if ringed:
        (tok_out,) = gather_products((activations,), in_block, 0)
    else:
        tok_out = product(activations, all_rows(in_block))

    keep = 1.0 - forget_mask.astype(jnp.float32)
    weights = look_up(importance, token_ids) * keep / total
    forget_grads = out_grads * forget_mask.astype(low)[:, None]
    grad_scale = 1.0 / math.sqrt(total)
    scaled = (tok_out * weights[:, None]).astype(low)
    forget_grads, scaled = lax.optimization_barrier((forget_grads, scaled))
    start = -rows_sum(forget_grads, grad_scale, 1)
    start, scaled = lax.optimization_barrier((start, scaled))
    both_block = rows_sum(scaled, 1.0, 2)
    both_block = (both_block + damping * in_block.astype(jnp.float32)).astype(low)
    both = all_columns(both_block)

    def mix(matrix):
        return product(all_columns(matrix.astype(low)), out_inverse).astype(low)

    if ringed:
        wide = all_columns(start.astype(low))
        precond_0, mixed = gather_products((in_inverse,), wide, 3, right=out_inverse, keep=True)
    else:
        mixed = all_rows(mix(start))
        precond_0 = product(in_inverse, mixed)
    if ringed and lax.axis_size("fac") == 4:
        image_0, mixed = spread(both, mixed, out_inverse, 4)
    else:
        image_0 = product(both, mixed)
        mixed = mix(image_0)
    if ringed:
        precond_1, image_1 = gather_products((in_inverse, both), mixed, 5)
    else:
        mixed = all_rows(mixed)
        precond_1 = product(in_inverse, mixed)
        image_1 = product(both, mixed)

    return finish((start, precond_0, image_0, precond_1, image_1), 6)


def solution(mesh):
    placed = (
        P("fsdp", None),
        P("fsdp", "fac"),
        P("fsdp"),
        P("fsdp"),
        P(),
        P("fsdp", None),
        P(None, "fac"),
    )
    return jax.shard_map(
        body,
        mesh=mesh,
        in_specs=placed,
        out_specs=(P("fsdp", "fac"), P("fsdp", "fac")),
        check_vma=False,
    )
```

```python
import functools
import math

import jax
import jax.numpy as jnp
from jax import lax
from jax.experimental import pallas as pl
from jax.experimental.pallas import tpu as pltpu
from jax.sharding import PartitionSpec as P

damping = 0.3
MESH = pl.DeviceIdType.MESH
VMEM_BYTES = 16 * 1024 * 1024


def product(left, right):
    return jnp.dot(left, right, preferred_element_type=jnp.float32)


def transposed_term(matrix, right):
    return lax.dot_general(
        matrix, right, (((0,), (0,)), ((), ())), preferred_element_type=jnp.float32
    )


def index_at(place, n):
    odd = place // (n // 2)
    return 2 * (place + odd * (n - 1 - 2 * place)) + odd


def ring(n):
    me = lax.axis_index("fsdp")
    pair = me // 2
    place = pair + (me % 2) * (n - 1 - 2 * pair)
    return me, place, index_at((place + 1) % n, n), index_at((place + n - 1) % n, n)


def greet(neighbours):
    barrier = pltpu.get_barrier_semaphore()
    for neighbour in neighbours:
        pl.semaphore_signal(barrier, inc=1, device_id=neighbour, device_id_type=MESH)
    pl.semaphore_wait(barrier, len(neighbours))


def gather_kernel(n, lefts, mixing, *refs):
    left_refs, block_ref, refs = refs[:lefts], refs[lefts], refs[lefts + 1 :]
    if mixing:
        right_ref, refs = refs[0], refs[1:]
    product_refs, full_ref = refs[:lefts], refs[lefts]
    send_sem, recv_sem = refs[lefts + 1 :]
    rows, columns = full_ref.shape[0] // n, full_ref.shape[1]
    half, piece = columns // 2, rows // 2
    me, place, following, preceding = ring(n)
    greet(({"fsdp": following}, {"fsdp": preceding}))

    def owner_at(step, way):
        return index_at((place + n - step) % n if way == 0 else (place + step) % n, n)

    def copy(step, way, part):
        at = full_ref.at[
            pl.ds(pl.multiple_of(owner_at(step, way) * rows + part * piece, piece), piece),
            pl.ds(way * half, half),
        ]
        return pltpu.make_async_remote_copy(
            src_ref=at,
            dst_ref=at,
            send_sem=send_sem.at[step, way, part],
            recv_sem=recv_sem.at[step, way, part],
            device_id={"fsdp": following if way == 0 else preceding},
            device_id_type=MESH,
        )

    for part in range(2):
        for way in range(2):
            lines, lanes = slice(part * piece, (part + 1) * piece), slice(way * half, (way + 1) * half)
            if mixing:
                block = product(block_ref[lines, :], right_ref[:, lanes]).astype(full_ref.dtype)
            else:
                block = block_ref[lines, lanes]
            full_ref[pl.ds(pl.multiple_of(me * rows + part * piece, piece), piece), lanes] = block
            copy(0, way, part).start()
    for ref in product_refs:
        ref[...] = jnp.zeros_like(ref)

    def step_body(step, carry):
        for way in range(2):
            for part in range(2):

                @pl.when(step > 0)
                def _():
                    copy(step - 1, way, part).wait_recv()

                @pl.when((step > 0) & (step < n - 1))
                def _():
                    copy(step, way, part).start()

        for way in range(2):
            at = pl.ds(pl.multiple_of(owner_at(step, way) * rows, rows), rows)
            block = full_ref[at, way * half : (way + 1) * half]
            for left_ref, ref in zip(left_refs, product_refs):
                ref[:, way * half : (way + 1) * half] += product(left_ref[:, at], block)
        return carry

    lax.fori_loop(0, n, step_body, 0)

    def settle(step, carry):
        for way in range(2):
            for part in range(2):
                copy(step, way, part).wait_send()
        return carry

    lax.fori_loop(0, n - 1, settle, 0)


def gather_products(lefts, block, number, right=None, keep=False):
    n = lax.axis_size("fsdp")
    rows, columns = block.shape[0], (block if right is None else right).shape[1]
    operands = (*lefts, block) if right is None else (*lefts, block, right)
    vmem = pl.BlockSpec(memory_space=pltpu.VMEM)
    outs = [jax.ShapeDtypeStruct((left.shape[0], columns), jnp.float32) for left in lefts]
    scratch = [pltpu.SemaphoreType.DMA((n - 1, 2, 2))] * 2
    if keep:
        outs.append(jax.ShapeDtypeStruct((n * rows, columns), block.dtype))
    else:
        scratch.insert(0, pltpu.VMEM((n * rows, columns), block.dtype))
    return pl.pallas_call(
        functools.partial(gather_kernel, n, len(lefts), right is not None),
        out_shape=outs,
        in_specs=[vmem] * len(operands),
        out_specs=[vmem] * len(outs),
        scratch_shapes=scratch,
        compiler_params=pltpu.CompilerParams(
            collective_id=number, has_side_effects=True, vmem_limit_bytes=VMEM_BYTES
        ),
        cost_estimate=pl.CostEstimate(
            flops=2 * n * rows * columns * sum(left.shape[0] for left in lefts),
            bytes_accessed=2 * n * rows * columns * 8,
            transcendentals=0,
        ),
    )(*operands)


def scatter_kernel(n, factor, left_ref, right_ref, out_ref, own, sent, held, send_sem, recv_sem):
    rows, columns = out_ref.shape
    half, piece = columns // 2, rows // 2
    me, place, following, preceding = ring(n)
    greet(({"fsdp": following}, {"fsdp": preceding}))

    def copy(step, way, part):
        return pltpu.make_async_remote_copy(
            src_ref=sent.at[step, way, part],
            dst_ref=held.at[step, way, part],
            send_sem=send_sem.at[step, way, part],
            recv_sem=recv_sem.at[step, way, part],
            device_id={"fsdp": following if way == 0 else preceding},
            device_id_type=MESH,
        )

    def step_body(step, carry):
        for way in range(2):
            target = index_at((place + 2 * n - 1 - step) % n if way == 0 else (place + 1 + step) % n, n)
            at = pl.ds(pl.multiple_of(target * rows, rows), rows)
            own[way] = transposed_term(left_ref[:, at], right_ref[:, way * half : (way + 1) * half])
        for part in range(2):
            for way in range(2):
                lines = slice(part * piece, (part + 1) * piece)

                @pl.when(step == 0)
                def _():
                    sent[step, way, part] = (own[way, lines, :] * factor).astype(sent.dtype)

                @pl.when(step > 0)
                def _():
                    copy(step - 1, way, part).wait_recv()
                    term = held[step - 1, way, part].astype(jnp.float32)
                    term = term + own[way, lines, :] * factor

                    @pl.when(step < n - 1)
                    def _():
                        sent[step, way, part] = term.astype(sent.dtype)

                    @pl.when(step == n - 1)
                    def _():
                        out_ref[lines, way * half : (way + 1) * half] = term

                @pl.when(step < n - 1)
                def _():
                    copy(step, way, part).start()

        return carry

    lax.fori_loop(0, n, step_body, 0)

    def settle(step, carry):
        for way in range(2):
            for part in range(2):
                copy(step, way, part).wait_send()
        return carry

    lax.fori_loop(0, n - 1, settle, 0)


def scatter_term(left, right, factor, number):
    n = lax.axis_size("fsdp")
    rows, columns = left.shape[1] // n, right.shape[1]
    vmem = pl.BlockSpec(memory_space=pltpu.VMEM)
    slots = pltpu.VMEM((n - 1, 2, 2, rows // 2, columns // 2), jnp.bfloat16)
    return pl.pallas_call(
        functools.partial(scatter_kernel, n, factor),
        out_shape=jax.ShapeDtypeStruct((rows, columns), jnp.float32),
        in_specs=[vmem] * 2,
        out_specs=vmem,
        scratch_shapes=[
            pltpu.VMEM((2, rows, columns // 2), jnp.float32),
            slots,
            slots,
            pltpu.SemaphoreType.DMA((n - 1, 2, 2)),
            pltpu.SemaphoreType.DMA((n - 1, 2, 2)),
        ],
        compiler_params=pltpu.CompilerParams(
            collective_id=number, has_side_effects=True, vmem_limit_bytes=VMEM_BYTES
        ),
        cost_estimate=pl.CostEstimate(
            flops=2 * left.shape[0] * left.shape[1] * columns,
            bytes_accessed=2 * n * rows * columns * 8,
            transcendentals=0,
        ),
    )(left, right)


def spread_kernel(both_ref, mixed_ref, right_ref, image_ref, out_ref, held, send_sem, recv_sem):
    rows, columns = image_ref.shape
    piece = rows // 2
    me = lax.axis_index("fac")
    beside = {"fac": me + 1 - 2 * (me % 2)}
    across = {"fac": (me + 2) % 4}
    greet((beside, across))

    def copy(number, part):
        source, slot, to = ((0, 1, beside), (0, 2, across), (2, 3, beside))[number]
        return pltpu.make_async_remote_copy(
            src_ref=held.at[source, part],
            dst_ref=held.at[slot, part],
            send_sem=send_sem.at[number, part],
            recv_sem=recv_sem.at[number, part],
            device_id=to,
            device_id_type=MESH,
        )

    def add(slot, owner):
        at = pl.ds(pl.multiple_of(owner * columns, columns), columns)
        for part in range(2):
            term = product(held[slot, part], right_ref[at, :])
            lines = slice(part * piece, (part + 1) * piece)
            image = term if slot == 0 else term + total[part]
            total[part] = image
            if slot == 3:
                out_ref[lines, :] = image.astype(out_ref.dtype)

    total = [None, None]
    for part in range(2):
        lines = slice(part * piece, (part + 1) * piece)
        image_ref[lines, :] = product(both_ref[lines, :], mixed_ref[...])
        held[0, part] = image_ref[lines, :].astype(held.dtype)
        copy(1, part).start()
        copy(0, part).start()
    add(0, me)
    for part in range(2):
        copy(0, part).wait_recv()
    add(1, me + 1 - 2 * (me % 2))
    for part in range(2):
        copy(1, part).wait_recv()
        copy(2, part).start()
    add(2, (me + 2) % 4)
    for part in range(2):
        copy(2, part).wait_recv()
    add(3, (me + 1 - 2 * (me % 2) + 2) % 4)
    for number in range(3):
        for part in range(2):
            copy(number, part).wait_send()


def spread(both, mixed, right, number):
    rows, columns = both.shape[0], mixed.shape[1]
    vmem = pl.BlockSpec(memory_space=pltpu.VMEM)
    return pl.pallas_call(
        spread_kernel,
        out_shape=(
            jax.ShapeDtypeStruct((rows, columns), jnp.float32),
            jax.ShapeDtypeStruct((rows, columns), jnp.bfloat16),
        ),
        in_specs=[vmem] * 3,
        out_specs=(vmem, vmem),
        scratch_shapes=[
            pltpu.VMEM((4, 2, rows // 2, columns), jnp.bfloat16),
            pltpu.SemaphoreType.DMA((3, 2)),
            pltpu.SemaphoreType.DMA((3, 2)),
        ],
        compiler_params=pltpu.CompilerParams(
            collective_id=number, has_side_effects=True, vmem_limit_bytes=VMEM_BYTES
        ),
        cost_estimate=pl.CostEstimate(
            flops=2 * rows * columns * (both.shape[1] + right.shape[0]),
            bytes_accessed=2 * (mixed.size + right.size),
            transcendentals=0,
        ),
    )(both, mixed, right)


PAIRS = ((0, 1), (1, 2), (0, 3), (2, 3), (1, 4), (3, 4))


def finish_kernel(sizes, *refs):
    blocks, outs = refs[:5], refs[5:7]
    sent, held, send_sem, recv_sem = refs[7:]
    rows, columns = outs[0].shape

    stages = []
    for axis, size in sizes:
        me = lax.axis_index(axis)
        stages.append([{axis: (me + away) % size} for away in range(1, size)])
    greet(stages[0] + stages[1])

    def lines_at(row):
        return pl.ds(pl.multiple_of(row * 8, 8), 8)

    def add_row(row, sums):
        values = [ref[lines_at(row), :] for ref in blocks]
        return tuple(total + values[a] * values[b] for total, (a, b) in zip(sums, PAIRS))

    sums = lax.fori_loop(0, rows // 8, add_row, (jnp.zeros((8, columns), jnp.float32),) * len(PAIRS))
    sums = [sum(one[:, lane : lane + 128] for lane in range(0, columns, 128)) for one in sums]
    slot = 0
    for stage, peers in enumerate(stages):
        for number, one in enumerate(sums):
            sent[stage, number] = one
        copies = []
        for peer in peers:
            copies.append(
                pltpu.make_async_remote_copy(
                    src_ref=sent.at[stage],
                    dst_ref=held.at[slot],
                    send_sem=send_sem.at[slot],
                    recv_sem=recv_sem.at[slot],
                    device_id=peer,
                    device_id_type=MESH,
                )
            )
            copies[-1].start()
            slot += 1
        for place, one in enumerate(copies):
            one.wait()
            at = slot - len(copies) + place
            sums = [total + held[at, number] for number, total in enumerate(sums)]

    rz, energy, rq, wq, zv, qv = [jnp.sum(one, axis=(0, 1), keepdims=True) for one in sums]
    alpha = rz / energy
    rz_new = rz - alpha * (energy + rq) + alpha * alpha * wq
    grow = 1.0 + rz_new / rz
    energy_new = grow * grow * energy - grow * alpha * (zv + wq) + alpha * alpha * qv
    alpha_new = rz_new / energy_new
    first = jnp.broadcast_to(alpha + alpha_new * grow, (8, columns))
    second = jnp.broadcast_to(alpha * alpha_new, (8, columns))

    def write_row(row, carry):
        at = lines_at(row)
        start, precond_0, image_0, precond_1, image_1 = [ref[at, :] for ref in blocks]
        outs[0][at, :] = first * precond_0 - second * precond_1
        outs[1][at, :] = start - first * image_0 + second * image_1
        return carry

    lax.fori_loop(0, rows // 8, write_row, 0)


def finish(blocks, number):
    sizes = [(axis, lax.axis_size(axis)) for axis in ("fac", "fsdp")]
    peers = sum(size - 1 for _, size in sizes)
    vmem = pl.BlockSpec(memory_space=pltpu.VMEM)
    shape = jax.ShapeDtypeStruct(blocks[0].shape, jnp.float32)
    return pl.pallas_call(
        functools.partial(finish_kernel, sizes),
        out_shape=(shape, shape),
        in_specs=[vmem] * 5,
        out_specs=(vmem, vmem),
        scratch_shapes=[
            pltpu.VMEM((2, len(PAIRS), 8, 128), jnp.float32),
            pltpu.VMEM((peers, len(PAIRS), 8, 128), jnp.float32),
            pltpu.SemaphoreType.DMA((peers,)),
            pltpu.SemaphoreType.DMA((peers,)),
        ],
        compiler_params=pltpu.CompilerParams(
            collective_id=number, has_side_effects=True, vmem_limit_bytes=VMEM_BYTES
        ),
    )(*blocks)


def look_up(table, ids):
    fold = 256
    if table.shape[0] % fold:
        return table[ids]
    folded = table.reshape(-1, fold)
    row, lane = ids[:, None] // fold, ids[:, None] % fold
    chosen = (row == jnp.arange(folded.shape[0])).astype(jnp.float32)
    near = jnp.dot(chosen, folded, precision=lax.Precision.HIGHEST)
    return jnp.sum(jnp.where(lane == jnp.arange(fold), near, 0.0), axis=1)


def body(activations, out_grads, token_ids, forget_mask, importance, in_inverse, out_inverse):
    low = jnp.bfloat16
    tok_rows = activations.shape[0]
    total = tok_rows * lax.axis_size("fsdp")
    columns = out_inverse.shape[1]
    own = lax.axis_index("fac") * columns

    shards = lax.axis_size("fsdp")
    rows = in_inverse.shape[0]
    ringed = shards % 2 == 0 and rows % 128 == 0 and columns % 256 == 0

    def rows_sum(right, factor, number):
        if ringed:
            return scatter_term(activations, right, factor, number)
        partial = (transposed_term(activations, right) * factor).astype(low)
        partial = lax.psum_scatter(partial, "fsdp", scatter_dimension=0, tiled=True)
        return partial.astype(jnp.float32)

    def all_rows(block):
        return lax.all_gather(block, "fsdp", axis=0, tiled=True)

    def all_columns(block):
        return lax.all_gather(block, "fac", axis=1, tiled=True)

    in_block = lax.dynamic_slice(in_inverse, (0, own), (in_inverse.shape[0], columns))
    if ringed:
        (tok_out,) = gather_products((activations,), in_block, 0)
    else:
        tok_out = product(activations, all_rows(in_block))

    keep = 1.0 - forget_mask.astype(jnp.float32)
    weights = look_up(importance, token_ids) * keep / total
    forget_grads = out_grads * forget_mask.astype(low)[:, None]
    grad_scale = 1.0 / math.sqrt(total)
    scaled = (tok_out * weights[:, None]).astype(low)
    forget_grads, scaled = lax.optimization_barrier((forget_grads, scaled))
    start = -rows_sum(forget_grads, grad_scale, 1)
    start, scaled = lax.optimization_barrier((start, scaled))
    both_block = rows_sum(scaled, 1.0, 2)
    both_block = (both_block + damping * in_block.astype(jnp.float32)).astype(low)
    both = all_columns(both_block)

    def mix(matrix):
        return product(all_columns(matrix.astype(low)), out_inverse).astype(low)

    if ringed:
        wide = all_columns(start.astype(low))
        precond_0, mixed = gather_products((in_inverse,), wide, 3, right=out_inverse, keep=True)
    else:
        mixed = all_rows(mix(start))
        precond_0 = product(in_inverse, mixed)
    if ringed and lax.axis_size("fac") == 4:
        image_0, mixed = spread(both, mixed, out_inverse, 4)
    else:
        image_0 = product(both, mixed)
        mixed = mix(image_0)
    if ringed:
        precond_1, image_1 = gather_products((in_inverse, both), mixed, 5)
    else:
        mixed = all_rows(mixed)
        precond_1 = product(in_inverse, mixed)
        image_1 = product(both, mixed)

    return finish((start, precond_0, image_0, precond_1, image_1), 6)


def solution(mesh):
    placed = (
        P("fsdp", None),
        P("fsdp", "fac"),
        P("fsdp"),
        P("fsdp"),
        P(),
        P("fsdp", None),
        P(None, "fac"),
    )
    return jax.shard_map(
        body,
        mesh=mesh,
        in_specs=placed,
        out_specs=(P("fsdp", "fac"), P("fsdp", "fac")),
        check_vma=False,
    )
```
